128 devices in a mesh: role: 2 (over z_hi), head: 4 (over z_lo, core), ctx: 16 (over y, x).
Axes of the slice: x: 4, y: 4, z: 4 (z_hi: 2, z_lo: 2; z = z_hi * 2 + z_lo), core: 2. Of those that a mesh axis runs over, the one named last changes fastest.
Arguments:
- history: bfloat16 [2, 2, 4096, 2048], P('role', None, 'ctx'), may hold values from -6 to 6
- queries: bfloat16 [2, 2, 1024, 2048], P('role', None, None, 'head'), may hold values from -150 to 150
- w_kv: bfloat16 [2048, 2, 16, 128], P(None, None, None, 'head'), may hold values from -0.125 to 0.125
- gain: float32 [2048], replicated, may hold values from 0.1 to 1.9
- w_out: bfloat16 [2048, 2048], P('head'), may hold values from -0.5 to 0.5
Outputs:
- attended: bfloat16 [2, 2, 1024, 2048], P('role', None, 'ctx', 'head')
The draws below stay inside these ranges and needn't reach their ends.
All inputs are finite; a program needn't handle non-finite values.
Results may differ from the reference program's by a relative error of at most 0.02.
The reference program's roundings to bfloat16 on the way count: a program that leaves them out, or rounds other values in their place, can miss the bound.
Values may be sent and summed in bfloat16 or wider, within the bound.
A program may use at most 256 MiB of HBM per device.

```python
import math
import jax
import jax.numpy as jnp
from jax import lax

D = 2048
H = 16
HD = 128
NQ = 1024
SEGS_HALF = 2
KEYS_DEV = 256
SEGMENT = 4096
N_CTX = 16


def draw_queries(key, part):
    key = jax.random.fold_in(key, 11)
    first_key = jax.random.fold_in(key, 0)
    shape = (2, SEGS_HALF, NQ, H * HD)
    values = jax.random.normal(first_key, shape, jnp.float32) * 2.0
    return jnp.clip(values, -150.0, 150.0).astype(jnp.bfloat16)


def levels(key, extent, cuts, low, high):
    def one(dim, shards_of):
        draws = jax.random.uniform(jax.random.fold_in(jax.random.fold_in(key, 6), dim), (shards_of,), jnp.float32, low / len(cuts), high / len(cuts))
        return jnp.repeat(jnp.exp(draws), extent[dim] // shards_of).reshape((-1,) + (1,) * (len(extent) - dim - 1))

    factor_of = one(*cuts[0])
    for cut in cuts[1:]:
        factor_of = factor_of * one(*cut)
    return factor_of


def centred(stream_key, extent, width, limit, shards=(), kind=jnp.bfloat16):
    drawn = width * jax.random.normal(stream_key, extent, jnp.float32)
    if shards:
        drawn = drawn * levels(stream_key, extent, shards, -0.22, 0.18)
    return jnp.clip(drawn, -limit, limit).astype(kind)


def setup_inputs(seed: int = 0) -> dict:
    keys = jax.random.split(jax.random.key(seed), 6)
    return {
        "history": centred(keys[0], (2, SEGS_HALF, SEGMENT, D), 1.0, 6.0, ((0, 2), (2, 16))),
        "queries": draw_queries(jax.random.fold_in(keys[5], 71), 0),
        "w_kv": centred(keys[2], (D, 2, H, HD), D ** -0.5, 0.125, ((3, 4),)),
        "gain": jnp.clip(1.0 + 0.18 * jax.random.normal(keys[3], (D,), jnp.float32), 0.1, 1.9),
        "w_out": centred(keys[4], (H * HD, D), (H * HD // 16) ** -0.5, 0.5, ((0, 4),)),
    }


def project_rows(row_data, gain, w_kv):
    values = row_data.astype(jnp.float32)
    mean_sq = lax.optimization_barrier(jnp.mean(values * values, axis=-1, keepdims=True))
    normed = (values * lax.rsqrt(mean_sq + 1e-05) * gain).astype(jnp.bfloat16)
    flat = w_kv.reshape(D, 2 * H * HD)
    packed = jnp.dot(normed, flat, preferred_element_type=jnp.float32).astype(jnp.bfloat16)
    return packed.reshape(-1, 2, H, HD)

def merge_parts(left_part, right_part):
    peak_left, total_left, accum_left = left_part
    peak_right, total_right, accum_right = right_part
    global_peak = jnp.maximum(peak_left, peak_right)
    scale_left = jnp.exp(peak_left - global_peak)
    scale_right = jnp.exp(peak_right - global_peak)
    merged_total = total_left * scale_left + total_right * scale_right
    merged_accum = accum_left * scale_left[..., None] + accum_right * scale_right[..., None]
    return (global_peak, merged_total, merged_accum)

def attend(query_rows, kv_rows, w_out):
    query_all = query_rows.astype(jnp.float32).reshape(NQ, H, HD)
    blocks = kv_rows.reshape(N_CTX, KEYS_DEV, 2, H, HD)
    score_scale = 1.0 / math.sqrt(HD)

    def step(carry, kv_block):
        key_rows = kv_block[:, 0].astype(jnp.float32)
        value_rows = kv_block[:, 1].astype(jnp.float32)
        scores = jnp.einsum('qne,tne->nqt', query_all, key_rows, precision=lax.Precision.HIGHEST) * score_scale
        row_peak = lax.optimization_barrier(jnp.max(scores, axis=-1))
        probability = jnp.exp(scores - row_peak[..., None]).astype(jnp.bfloat16)
        probability = lax.optimization_barrier(probability).astype(jnp.float32)
        row_total = lax.optimization_barrier(jnp.sum(probability, axis=-1))
        row_accum = jnp.einsum('nqt,tne->nqe', probability, value_rows, precision=lax.Precision.HIGHEST)
        return (merge_parts(carry, (row_peak, row_total, row_accum)), None)
    start_state = (jnp.full((H, NQ), -1e+30, jnp.float32), jnp.zeros((H, NQ), jnp.float32), jnp.zeros((H, NQ, HD), jnp.float32))
    final_state, unused = lax.scan(step, start_state, blocks)
    global_peak, row_total, row_accum = final_state
    heads_out = (row_accum / row_total[..., None]).transpose(1, 0, 2).reshape(NQ, H * HD).astype(jnp.bfloat16)
    return jnp.dot(heads_out, w_out, preferred_element_type=jnp.float32).astype(jnp.bfloat16)

def reference(history, queries, w_kv, gain, w_out):
    projected = [[project_rows(history[role_index, segment], gain, w_kv) for segment in range(SEGS_HALF)] for role_index in range(2)]
    results = []
    for role_index in range(2):
        stacked = [attend(queries[role_index, segment], projected[1 - role_index][segment], w_out) for segment in range(SEGS_HALF)]
        results.append(jnp.stack(stacked))
    return jnp.stack(results)
```

```python
import math

import jax
import jax.numpy as jnp
from jax import lax
from jax.experimental import pallas as pl
from jax.experimental.pallas import tpu as pltpu
from jax.sharding import PartitionSpec as P

MESH = pl.DeviceIdType.MESH
HD = 128
D = 2048
CHUNKS = 4
KEYS = 256
ROWS = 64
SCALE = math.log2(math.e) / math.sqrt(HD)
NT = (((1,), (1,)), ((), ()))


def merge(parts):
    top = parts[0][1]
    for _, peak, _ in parts[1:]:
        top = jnp.maximum(top, peak)
    accum = total = None
    for part, peak, part_total in parts:
        weight = jnp.exp2((peak - top) * SCALE)
        add = part.astype(jnp.float32) * weight
        accum = add if accum is None else accum + add
        add = part_total * weight
        total = add if total is None else total + add
    return accum, top, total


def kernel(
    hist, quer, w_kv, gain, w_out, out,
    x_buf, xn_buf, g_buf, w_buf, q_buf, wo_buf,
    kv_out, kv_in, a_out, a_ml, a_in, a_in_ml, b_out, b_ml, b_in, b_in_ml,
    p_acc, p_out, p_in,
    x_sem, g_sem, w_sem, q_sem, wo_sem,
    kv_ss, kv_rs, a_ss, a_rs, b_ss, b_rs, p_ss, p_rs,
):
    role, head, ctx = lax.axis_index("role"), lax.axis_index("head"), lax.axis_index("ctx")
    core = head % 2
    x, y = ctx % 4, ctx // 4
    first = (1 - core) * x + core * y
    second = (1 - core) * y + core * x

    def ctx_of(f, g):
        return f * (1 + 3 * core) + g * (4 - 3 * core)

    def a_peer(d):
        return role, head, ctx_of((first + d) % 4, second)

    def b_peer(d):
        return role, head, ctx_of(first, (second + d) % 4)

    def h_peer(d):
        return role, (head + d) % 4, ctx

    barrier = pltpu.get_barrier_semaphore()
    peers = [(1 - role, other, ctx) for other in range(4)]
    for d in range(1, 4):
        peers += [a_peer(d), b_peer(d), h_peer(d)]
    for peer in peers:
        pl.semaphore_signal(barrier, inc=1, device_id=peer, device_id_type=MESH)

    g_copy = pltpu.make_async_copy(gain, g_buf, g_sem)
    g_copy.start()
    x_copies = [pltpu.make_async_copy(hist.at[s], x_buf.at[s], x_sem.at[s]) for s in range(2)]
    for copy in x_copies:
        copy.start()
    w_copies = [
        [pltpu.make_async_copy(w_kv.at[k, :, j], w_buf.at[j, :, k], w_sem.at[j, k]) for k in range(2)]
        for j in range(CHUNKS)
    ]
    for pair in w_copies:
        for copy in pair:
            copy.start()
    q_copies = []
    for s in range(2):
        for f in range(4):
            for g in range(4):
                place = g if s == 0 else g ^ 1
                q_copies.append(
                    pltpu.make_async_copy(
                        quer.at[s, ctx_of(f, g)],
                        q_buf.at[s, f, pl.ds(place * ROWS, ROWS)],
                        q_sem.at[s, f, g],
                    )
                )
    for copy in q_copies:
        copy.start()
    wo_copy = pltpu.make_async_copy(w_out, wo_buf, wo_sem)
    wo_copy.start()

    g_copy.wait()
    for s in range(2):
        x_copies[s].wait()

        def norm(i, carry):
            rows = pl.ds(i * 32, 32)
            values = x_buf[s, rows, :].astype(jnp.float32)
            mean_sq = jnp.mean(values * values, axis=-1, keepdims=True)
            normed = values * lax.rsqrt(mean_sq + 1e-05) * g_buf[...]
            xn_buf[pl.ds(s * KEYS + i * 32, 32), :] = normed.astype(jnp.bfloat16)
            return carry

        lax.fori_loop(0, KEYS // 32, norm, 0)

    def kv_copy(j, other, slot):
        return pltpu.make_async_remote_copy(
            src_ref=kv_out.at[j, other],
            dst_ref=kv_in.at[j, :, pl.ds(pl.multiple_of(slot * 32, 32), 32), :],
            send_sem=kv_ss.at[j, other],
            recv_sem=kv_rs.at[j, slot],
            device_id=(1 - role, other, ctx),
            device_id_type=MESH,
        )

    sends = []
    for j in range(CHUNKS):
        for copy in w_copies[j]:
            copy.wait()
        projected = lax.dot_general(
            w_buf[j].reshape(256, D), xn_buf[...], NT, preferred_element_type=jnp.float32
        )
        kv_out[j] = projected.astype(jnp.bfloat16).reshape(4, 2, 32, 2 * KEYS)
        if j == 0:
            pl.semaphore_wait(barrier, len(peers))
        for other in range(4):
            copy = kv_copy(j, other, head)
            copy.start()
            sends.append(copy)

    for copy in q_copies:
        copy.wait()

    low = lax.broadcasted_iota(jnp.int32, (1, HD), 1) < ROWS
    ones = jnp.ones((16, KEYS), jnp.bfloat16)

    def interleave(left, right):
        pieces = []
        for p in range(2):
            lanes = slice(p * HD, (p + 1) * HD)
            pieces += [
                jnp.where(low, left[:, lanes], right[:, lanes]),
                jnp.where(low, right[:, lanes], left[:, lanes]),
            ]
        return jnp.concatenate(pieces, axis=1)

    def a_copies(j, d):
        f = (first + d) % 4
        return [
            pltpu.make_async_remote_copy(
                src_ref=src.at[j, f],
                dst_ref=dst.at[j, d - 1],
                send_sem=a_ss.at[j, d - 1, i],
                recv_sem=a_rs.at[j, d - 1, i],
                device_id=a_peer(d),
                device_id_type=MESH,
            )
            for i, (src, dst) in enumerate(((a_out, a_in), (a_ml, a_in_ml)))
        ]

    def b_copies(j, d):
        g = (second + d) % 4
        return [
            pltpu.make_async_remote_copy(
                src_ref=src.at[j, g],
                dst_ref=dst.at[j, d - 1],
                send_sem=b_ss.at[j, d - 1, i],
                recv_sem=b_rs.at[j, d - 1, i],
                device_id=b_peer(d),
                device_id_type=MESH,
            )
            for i, (src, dst) in enumerate(((b_out, b_in), (b_ml, b_in_ml)))
        ]

    def attend(j):
        for slot in range(4):
            kv_copy(j, slot, slot).wait_recv()
        keys, values = [], []
        for s in range(2):
            lanes = slice(s * KEYS, (s + 1) * KEYS)
            keys.append(kv_in[j, 0, :, lanes].T)
            values.append(jnp.concatenate([kv_in[j, 1, :, lanes], ones], axis=0))
        for d in (2, 1, 3, 0):
            f = (first + d) % 4
            accums, peaks, totals = [], [], []
            for s in range(2):
                block = q_buf[s, f, :, j * HD : (j + 1) * HD]
                scores = lax.dot_general(keys[s], block, NT, preferred_element_type=jnp.float32)
                peak = jnp.max(scores, axis=0, keepdims=True)
                probability = jnp.exp2((scores - peak) * SCALE).astype(jnp.bfloat16)
                accum = jnp.dot(values[s], probability, preferred_element_type=jnp.float32)
                accums.append(accum[:HD])
                totals.append(accum[HD : HD + 1])
                peaks.append(peak)
            a_out[j, f] = interleave(*accums).astype(jnp.bfloat16)
            a_ml[j, f, 0:1] = interleave(*peaks)
            a_ml[j, f, 1:2] = interleave(*totals)
            if d:
                for copy in a_copies(j, d):
                    copy.start()
                    sends.append(copy)

    def merge_first(j):
        parts = [(a_out[j, first], a_ml[j, first, 0:1], a_ml[j, first, 1:2])]
        for d in range(1, 4):
            for copy in a_copies(j, d):
                copy.wait_recv()
            parts.append((a_in[j, d - 1], a_in_ml[j, d - 1, 0:1], a_in_ml[j, d - 1, 1:2]))
        accum, peak, total = merge(parts)
        accum = accum.astype(jnp.bfloat16)
        for g in range(4):
            lanes = slice(g * HD, (g + 1) * HD)
            b_out[j, g] = accum[:, lanes]
            b_ml[j, g, 0:1] = peak[:, lanes]
            b_ml[j, g, 1:2] = total[:, lanes]
        for d in range(1, 4):
            for copy in b_copies(j, d):
                copy.start()
                sends.append(copy)

    def merge_second(j):
        parts = [(b_out[j, second], b_ml[j, second, 0:1], b_ml[j, second, 1:2])]
        for d in range(1, 4):
            for copy in b_copies(j, d):
                copy.wait_recv()
            parts.append((b_in[j, d - 1], b_in_ml[j, d - 1, 0:1], b_in_ml[j, d - 1, 1:2]))
        accum, _, total = merge(parts)
        rows = (accum / total).T.astype(jnp.bfloat16)
        if j == 0:
            wo_copy.wait()
        for other in range(4):
            part = jnp.dot(
                rows,
                wo_buf[j * HD : (j + 1) * HD, other * 512 : (other + 1) * 512],
                preferred_element_type=jnp.float32,
            )
            if j:
                part = part + p_acc[other]
            p_acc[other] = part

    attend(0)
    for j in range(1, CHUNKS):
        attend(j)
        merge_first(j - 1)
        if j >= 2:
            merge_second(j - 2)
    merge_first(CHUNKS - 1)
    merge_second(CHUNKS - 2)
    merge_second(CHUNKS - 1)

    odd = second % 2
    for other in range(4):
        for p in range(2):
            p_out[other, (odd + p) % 2] = p_acc[other, p * ROWS : (p + 1) * ROWS].astype(jnp.bfloat16)
    p_copies = []
    for d in (2, 1, 3):
        copy = pltpu.make_async_remote_copy(
            src_ref=p_out.at[(head + d) % 4],
            dst_ref=p_in.at[d - 1],
            send_sem=p_ss.at[d - 1],
            recv_sem=p_rs.at[d - 1],
            device_id=h_peer(d),
            device_id_type=MESH,
        )
        copy.start()
        p_copies.append(copy)
    for copy in p_copies:
        copy.wait_recv()
    for p in range(2):
        place = (odd + p) % 2
        total = p_acc[head, p * ROWS : (p + 1) * ROWS]
        for d in range(3):
            total = total + p_in[d, place].astype(jnp.float32)
        out[0, place] = total.astype(jnp.bfloat16)
    for copy in sends + p_copies:
        copy.wait_send()


def local(history, queries, w_kv, gain, w_out):
    bf16, f32 = jnp.bfloat16, jnp.float32
    dma = pltpu.SemaphoreType.DMA
    hist = history.reshape(2, KEYS, D)
    quer = queries.reshape(2, 16, ROWS, 4 * HD)
    w_kv = jnp.transpose(w_kv, (1, 2, 3, 0)).reshape(2, 4, CHUNKS, 32, D)
    return pl.pallas_call(
        kernel,
        out_shape=jax.ShapeDtypeStruct((1, 2, ROWS, 512), bf16),
        in_specs=[pl.BlockSpec(memory_space=pl.ANY)] * 5,
        out_specs=pl.BlockSpec(memory_space=pltpu.VMEM),
        scratch_shapes=[
            pltpu.VMEM((2, KEYS, D), bf16),
            pltpu.VMEM((2 * KEYS, D), bf16),
            pltpu.VMEM((1, D), f32),
            pltpu.VMEM((CHUNKS, 4, 2, 32, D), bf16),
            pltpu.VMEM((2, 4, 4 * ROWS, 4 * HD), bf16),
            pltpu.VMEM((4 * HD, D), bf16),
            pltpu.VMEM((CHUNKS, 4, 2, 32, 2 * KEYS), bf16),
            pltpu.VMEM((CHUNKS, 2, HD, 2 * KEYS), bf16),
            pltpu.VMEM((CHUNKS, 4, HD, 512), bf16),
            pltpu.VMEM((CHUNKS, 4, 2, 512), f32),
            pltpu.VMEM((CHUNKS, 3, HD, 512), bf16),
            pltpu.VMEM((CHUNKS, 3, 2, 512), f32),
            pltpu.VMEM((CHUNKS, 4, HD, HD), bf16),
            pltpu.VMEM((CHUNKS, 4, 2, HD), f32),
            pltpu.VMEM((CHUNKS, 3, HD, HD), bf16),
            pltpu.VMEM((CHUNKS, 3, 2, HD), f32),
            pltpu.VMEM((4, 2 * ROWS, 512), f32),
            pltpu.VMEM((4, 2, ROWS, 512), bf16),
            pltpu.VMEM((3, 2, ROWS, 512), bf16),
            dma((2,)),
            dma,
            dma((CHUNKS, 2)),
            dma((2, 4, 4)),
            dma,
            dma((CHUNKS, 4)),
            dma((CHUNKS, 4)),
            dma((CHUNKS, 3, 2)),
            dma((CHUNKS, 3, 2)),
            dma((CHUNKS, 3, 2)),
            dma((CHUNKS, 3, 2)),
            dma((3,)),
            dma((3,)),
        ],
        compiler_params=pltpu.CompilerParams(
            collective_id=0, has_side_effects=True, vmem_limit_bytes=48 * 2**20
        ),
        cost_estimate=pl.CostEstimate(flops=6 * 10**9, bytes_accessed=10 * 2**20, transcendentals=2**21),
    )(hist, quer, w_kv, gain.reshape(1, D), w_out)


def solution(mesh):
    placed = (
        P("role", None, "ctx", None),
        P("role", None, None, "head"),
        P(None, None, None, "head"),
        P(),
        P("head", None),
    )
    return jax.shard_map(
        local, mesh=mesh, in_specs=placed, out_specs=P("role", None, "ctx", "head"), check_vma=False
    )
```

```python
import math

import jax
import jax.numpy as jnp
from jax import lax
from jax.experimental import pallas as pl
from jax.experimental.pallas import tpu as pltpu
from jax.sharding import PartitionSpec as P

MESH = pl.DeviceIdType.MESH
HD = 128
D = 2048
CHUNKS = 4
KEYS = 256
ORDER = (0, 1)
ROWS = 64
SCALE = math.log2(math.e) / math.sqrt(HD)
NT = (((1,), (1,)), ((), ()))


def merge(parts):
    top = parts[0][1]
    for _, peak, _ in parts[1:]:
        top = jnp.maximum(top, peak)
    accum = total = None
    for part, peak, part_total in parts:
        weight = jnp.exp2((peak - top) * SCALE)
        add = part.astype(jnp.float32) * weight
        accum = add if accum is None else accum + add
        add = part_total * weight
        total = add if total is None else total + add
    return accum, top, total


def kernel(
    hist, quer, w_kv, gain, w_out, out,
    x_buf, xn_buf, g_buf, w_buf, q_buf, wo_buf,
    kv_out, kv_in, a_out, a_ml, a_in, a_in_ml, b_out, b_ml, b_in, b_in_ml,
    t_buf, ho_buf, p_out, p_in0, p_in1,
    x_sem, g_sem, w_sem, q_sem, wo_sem,
    kv_ss, kv_rs, q_ss, q_rs, a_ss, a_rs, b_ss, b_rs, p0_ss, p0_rs, p1_ss, p1_rs,
):
    role, head, ctx = lax.axis_index("role"), lax.axis_index("head"), lax.axis_index("ctx")
    x, y = ctx % 4, ctx // 4
    place = (x, y)

    def peer_of(axis, d):
        return role, head, (4 * y + (x + d) % 4 if axis == 0 else 4 * ((y + d) % 4) + x)

    def h_peer(d):
        return role, (head + d) % 4, ctx

    def block(g):
        return pl.ds(pl.multiple_of(g * ROWS, ROWS), ROWS)

    def slices(slot):
        return pl.ds(pl.multiple_of(slot * 32, 32), 32)

    barrier = pltpu.get_barrier_semaphore()
    peers = [(1 - role, other, ctx) for other in range(4)]
    for d in range(1, 4):
        peers += [peer_of(0, d), peer_of(1, d), h_peer(d)]
    for peer in peers:
        pl.semaphore_signal(barrier, inc=1, device_id=peer, device_id_type=MESH)

    g_copy = pltpu.make_async_copy(gain, g_buf, g_sem)
    x_copies = [pltpu.make_async_copy(hist.at[s], x_buf.at[s], x_sem.at[s]) for s in range(2)]
    w_copies = [
        [pltpu.make_async_copy(w_kv.at[k, :, j], w_buf.at[j, :, k], w_sem.at[j, k]) for k in range(2)]
        for j in range(CHUNKS)
    ]
    quer_copy = pltpu.make_async_copy(quer.at[0], q_buf.at[0], q_sem)
    wo_copy = pltpu.make_async_copy(w_out, wo_buf, wo_sem)
    g_copy.start()
    x_copies[ORDER[0]].start()
    for pair in w_copies:
        for copy in pair:
            copy.start()
    x_copies[ORDER[1]].start()
    quer_copy.start()
    wo_copy.start()

    sends = []

    def send(copies):
        for copy in copies:
            copy.start()
            sends.append(copy)

    def norm(s):
        x_copies[s].wait()

        def rows_of(i, carry):
            rows = pl.ds(i * 64, 64)
            values = x_buf[s, rows, :].astype(jnp.float32)
            mean_sq = jnp.mean(values * values, axis=-1, keepdims=True)
            normed = values * lax.rsqrt(mean_sq + 1e-05) * g_buf[...]
            xn_buf[s, rows, :] = normed.astype(jnp.bfloat16)
            return carry

        lax.fori_loop(0, KEYS // 64, rows_of, 0)

    def kv_copy(s, j, other, slot):
        return pltpu.make_async_remote_copy(
            src_ref=kv_out.at[s, j, other],
            dst_ref=kv_in.at[s, j, :, slices(slot), :],
            send_sem=kv_ss.at[s, j, other],
            recv_sem=kv_rs.at[s, j, slot],
            device_id=(1 - role if s == 0 else role, other, ctx),
            device_id_type=MESH,
        )

    def project(s, chunks):
        for j in chunks:
            if s == ORDER[0]:
                for copy in w_copies[j]:
                    copy.wait()
            projected = lax.dot_general(
                w_buf[j].reshape(256, D), xn_buf[s], NT, preferred_element_type=jnp.float32
            )
            kv_out[s, j] = projected.astype(jnp.bfloat16).reshape(4, 2, 32, KEYS)
            if s == 0:
                send([kv_copy(s, j, (head + d) % 4, head) for d in (2, 3, 0, 1)])
            else:
                send([kv_copy(s, j, (head + d) % 4, head) for d in (2, 3, 1)])
                kv_in[s, j, :, slices(head), :] = kv_out[s, j, head]

    def q_copy(hop, i, src, dst, peer):
        return pltpu.make_async_remote_copy(
            src_ref=src,
            dst_ref=dst,
            send_sem=q_ss.at[hop, i],
            recv_sem=q_rs.at[hop, i],
            device_id=peer,
            device_id_type=MESH,
        )

    def q_hop(hop, half, d, back):
        columns = slice(half * 256, (half + 1) * 256)
        at = [x, y]
        axis = half if hop == 1 else 1 - half
        if back:
            at[axis] = (at[axis] + 4 - d) % 4
        if hop == 1:
            ref = q_buf.at[1, at[1], at[0], :, columns]
        elif half == 0:
            ref = q_buf.at[1, at[1], :, :, columns]
        else:
            ref = q_buf.at[1, :, at[0], :, columns]
        return q_copy(hop, 3 * half + d - 1, ref, ref, peer_of(axis, d))

    hops = [(half, d) for d in (2, 1, 3) for half in range(2)]
    q_first = q_copy(0, 0, quer.at[1, y, x], q_buf.at[1, y, x], (1 - role, head, ctx))
    a, b = ORDER
    pl.semaphore_wait(barrier, len(peers))
    send([q_first])
    g_copy.wait()
    norm(a)
    project(a, (0,))
    q_first.wait_recv()
    send([q_hop(1, half, d, False) for half, d in hops])
    project(a, (1, 2))
    for half, d in hops:
        q_hop(1, half, d, True).wait_recv()
    send([q_hop(2, half, d, False) for half, d in hops])
    project(a, (3,))
    norm(b)
    project(b, range(CHUNKS))

    ones = jnp.ones((16, KEYS), jnp.bfloat16)

    def a_copies(s, j, d):
        f = (place[j % 2] + d) % 4
        return [
            pltpu.make_async_remote_copy(
                src_ref=src.at[s, j, f],
                dst_ref=dst.at[s, j, d - 1],
                send_sem=a_ss.at[s, j, d - 1, i],
                recv_sem=a_rs.at[s, j, d - 1, i],
                device_id=peer_of(j % 2, d),
                device_id_type=MESH,
            )
            for i, (src, dst) in enumerate(((a_out, a_in), (a_ml, a_in_ml)))
        ]

    def b_copies(s, j, d):
        g = (place[1 - j % 2] + d) % 4 // 2
        return [
            pltpu.make_async_remote_copy(
                src_ref=src.at[s, j, g],
                dst_ref=dst.at[s, j, d - 1],
                send_sem=b_ss.at[s, j, d - 1, i],
                recv_sem=b_rs.at[s, j, d - 1, i],
                device_id=peer_of(1 - j % 2, d),
                device_id_type=MESH,
            )
            for i, (src, dst) in enumerate(((b_out, b_in), (b_ml, b_in_ml)))
        ]

    def wait_inputs(s, j):
        if j == 0:
            if s == 0:
                quer_copy.wait()
            else:
                for half, d in hops:
                    q_hop(2, half, d, True).wait_recv()
        for i in (j, j + 1):
            for d in range(4) if s == 0 else range(1, 4):
                slot = (head + d) % 4
                kv_copy(s, i, slot, slot).wait_recv()

    def attend(s, j):
        keys = kv_in[s, j, 0].T
        values = jnp.concatenate([kv_in[s, j, 1], ones], axis=0)
        columns = slice(j * HD, (j + 1) * HD)
        if j % 2:
            query_rows = q_buf[s, :, :, :, columns].reshape(4 * KEYS, HD)
        else:
            query_rows = jnp.concatenate([q_buf[s, :, g, :, columns].reshape(KEYS, HD) for g in range(4)], axis=0)
        scores = lax.dot_general(keys, query_rows, NT, preferred_element_type=jnp.float32)
        peak = jnp.max(scores, axis=0, keepdims=True)
        probability = jnp.exp2((scores - peak) * SCALE).astype(jnp.bfloat16)
        accum = jnp.dot(values, probability, preferred_element_type=jnp.float32)
        for f in range(4):
            lanes = slice(f * KEYS, (f + 1) * KEYS)
            a_out[s, j, f] = accum[:HD, lanes].astype(jnp.bfloat16)
            a_ml[s, j, f, 0:1] = peak[:, lanes]
            a_ml[s, j, f, 1:2] = accum[HD : HD + 1, lanes]

    def merge_first(s, j):
        own = place[j % 2]
        parts = [(a_out[s, j, own], a_ml[s, j, own, 0:1], a_ml[s, j, own, 1:2])]
        for d in range(3):
            parts.append((a_in[s, j, d], a_in_ml[s, j, d, 0:1], a_in_ml[s, j, d, 1:2]))
        accum, peak, total = merge(parts)
        accum = accum.astype(jnp.bfloat16)
        for g in range(2):
            lanes = slice(g * HD, (g + 1) * HD)
            b_out[s, j, g] = accum[:, lanes]
            b_ml[s, j, g, 0:1] = peak[:, lanes]
            b_ml[s, j, g, 1:2] = total[:, lanes]

    def merge_second(s, j):
        own = place[1 - j % 2] // 2
        parts = [(b_out[s, j, own], b_ml[s, j, own, 0:1], b_ml[s, j, own, 1:2])]
        for d in range(3):
            parts.append((b_in[s, j, d], b_in_ml[s, j, d, 0:1], b_in_ml[s, j, d, 1:2]))
        accum, _, total = merge(parts)
        t_buf[s, j] = (accum / total).T
        ho_buf[s, :, j * HD : (j + 1) * HD] = t_buf[s, j, block(place[1 - j % 2] % 2), :].astype(jnp.bfloat16)

    def exchange(copies, s, j):
        for d in (2, 1, 3):
            pairs = [copies(s, i, d) for i in (j, j + 1)]
            send([pair[n] for n in range(2) for pair in pairs])

    def arrive(copies, s, j):
        for i in (j, j + 1):
            for d in range(1, 4):
                for copy in copies(s, i, d):
                    copy.wait_recv()

    def p_copy(s, d, other, slot):
        src, dst, ss, rs = ((p_out.at[0], p_in0, p0_ss, p0_rs), (p_out.at[1], p_in1, p1_ss, p1_rs))[s]
        return pltpu.make_async_remote_copy(
            src_ref=src.at[other],
            dst_ref=dst.at[d],
            send_sem=ss.at[d],
            recv_sem=rs.at[d],
            device_id=(role if s == 0 else 1 - role, other, ctx),
            device_id_type=MESH,
        )

    def finish(s):
        if s == ORDER[0]:
            wo_copy.wait()
        for other in range(4):
            part = jnp.dot(
                ho_buf[s], wo_buf[:, other * 512 : (other + 1) * 512], preferred_element_type=jnp.float32
            )
            p_out[s, other] = part.astype(jnp.bfloat16)
        send([p_copy(s, d, (head + d) % 4, head) for d in ((2, 1, 3) if s == 0 else (2, 3, 0, 1))])

    pairs = [(s, j) for s in ORDER for j in (0, 2)]
    for u in range(6):
        if u < 4:
            s, j = pairs[u]
            wait_inputs(s, j)
            attend(s, j)
            attend(s, j + 1)
            exchange(a_copies, s, j)
        if 1 <= u <= 4:
            s, j = pairs[u - 1]
            arrive(a_copies, s, j)
            merge_first(s, j)
            merge_first(s, j + 1)
            exchange(b_copies, s, j)
        if u >= 2:
            s, j = pairs[u - 2]
            arrive(b_copies, s, j)
            merge_second(s, j)
            merge_second(s, j + 1)
        if u == 3:
            finish(ORDER[0])
    finish(ORDER[1])
    for s in ORDER:
        total = p_out[0, head].astype(jnp.float32) if s == 0 else None
        for d in range(1, 4) if s == 0 else range(4):
            p_copy(s, d, (head + d) % 4, head).wait_recv()
            part = (p_in0 if s == 0 else p_in1)[d].astype(jnp.float32)
            total = part if total is None else total + part
        out[0, s] = total.astype(jnp.bfloat16)
    for copy in sends:
        copy.wait_send()


def local(history, queries, w_kv, gain, w_out):
    bf16, f32 = jnp.bfloat16, jnp.float32
    dma = pltpu.SemaphoreType.DMA
    hist = history.reshape(2, KEYS, D)
    quer = queries.reshape(2, 4, 4, ROWS, 4 * HD)
    w_kv = jnp.transpose(w_kv, (1, 2, 3, 0)).reshape(2, 4, CHUNKS, 32, D)
    return pl.pallas_call(
        kernel,
        out_shape=jax.ShapeDtypeStruct((1, 2, ROWS, 512), bf16),
        in_specs=[pl.BlockSpec(memory_space=pl.ANY)] * 5,
        out_specs=pl.BlockSpec(memory_space=pltpu.VMEM),
        scratch_shapes=[
            pltpu.VMEM((2, KEYS, D), bf16),
            pltpu.VMEM((2, KEYS, D), bf16),
            pltpu.VMEM((1, D), f32),
            pltpu.VMEM((CHUNKS, 4, 2, 32, D), bf16),
            pltpu.VMEM((2, 4, 4, ROWS, 4 * HD), bf16),
            pltpu.VMEM((4 * HD, D), bf16),
            pltpu.VMEM((2, CHUNKS, 4, 2, 32, KEYS), bf16),
            pltpu.VMEM((2, CHUNKS, 2, HD, KEYS), bf16),
            pltpu.VMEM((2, CHUNKS, 4, HD, KEYS), bf16),
            pltpu.VMEM((2, CHUNKS, 4, 2, KEYS), f32),
            pltpu.VMEM((2, CHUNKS, 3, HD, KEYS), bf16),
            pltpu.VMEM((2, CHUNKS, 3, 2, KEYS), f32),
            pltpu.VMEM((2, CHUNKS, 2, HD, HD), bf16),
            pltpu.VMEM((2, CHUNKS, 2, 2, HD), f32),
            pltpu.VMEM((2, CHUNKS, 3, HD, HD), bf16),
            pltpu.VMEM((2, CHUNKS, 3, 2, HD), f32),
            pltpu.VMEM((2, CHUNKS, HD, HD), f32),
            pltpu.VMEM((2, ROWS, 4 * HD), bf16),
            pltpu.VMEM((2, 4, ROWS, 512), bf16),
            pltpu.VMEM((4, ROWS, 512), bf16),
            pltpu.VMEM((4, ROWS, 512), bf16),
            dma((2,)),
            dma,
            dma((CHUNKS, 2)),
            dma,
            dma,
            dma((2, CHUNKS, 4)),
            dma((2, CHUNKS, 4)),
            dma((3, 6)),
            dma((3, 6)),
            dma((2, CHUNKS, 3, 2)),
            dma((2, CHUNKS, 3, 2)),
            dma((2, CHUNKS, 3, 2)),
            dma((2, CHUNKS, 3, 2)),
            dma((4,)),
            dma((4,)),
            dma((4,)),
            dma((4,)),
        ],
        compiler_params=pltpu.CompilerParams(
            collective_id=0, has_side_effects=True, vmem_limit_bytes=60 * 2**20
        ),
        cost_estimate=pl.CostEstimate(flops=6 * 10**9, bytes_accessed=10 * 2**20, transcendentals=2**21),
    )(hist, quer, w_kv, gain.reshape(1, D), w_out)


def solution(mesh):
    placed = (
        P("role", None, "ctx", None),
        P("role", None, None, "head"),
        P(None, None, None, "head"),
        P(),
        P("head", None),
    )
    return jax.shard_map(
        local, mesh=mesh, in_specs=placed, out_specs=P("role", None, "ctx", "head"), check_vma=False
    )
```

```python
import math

import jax
import jax.numpy as jnp
from jax import lax
from jax.experimental import pallas as pl
from jax.experimental.pallas import tpu as pltpu
from jax.sharding import PartitionSpec as P

MESH = pl.DeviceIdType.MESH
HD = 128
D = 2048
CHUNKS = 4
KEYS = 256
AHEAD = 2
ROWS = 64
SCALE = math.log2(math.e) / math.sqrt(HD)
NT = (((1,), (1,)), ((), ()))


def merge(parts):
    top = parts[0][1]
    for _, peak, _ in parts[1:]:
        top = jnp.maximum(top, peak)
    accum = total = None
    for part, peak, part_total in parts:
        weight = jnp.exp2((peak - top) * SCALE)
        add = part.astype(jnp.float32) * weight
        accum = add if accum is None else accum + add
        add = part_total * weight
        total = add if total is None else total + add
    return accum, top, total


def kernel(
    hist, quer, w_kv, gain, w_out, out,
    x_buf, xn_buf, g_buf, w_buf, q_buf, wo_buf,
    kv_out, kv_in, a_out, a_ml, a_in, a_in_ml, b_out, b_ml, b_in, b_in_ml,
    t_buf, ho_buf, p_out, p_in,
    x_sem, g_sem, w_sem, q_sem, wo_sem,
    kv_ss, kv_rs, a_ss, a_rs, b_ss, b_rs, p_ss, p_rs,
):
    role, head, ctx = lax.axis_index("role"), lax.axis_index("head"), lax.axis_index("ctx")
    x, y = ctx % 4, ctx // 4
    core = head % 2

    def peer_of(axis, d):
        return role, head, 4 * ((y + d * axis) % 4) + (x + d * (1 - axis)) % 4

    def axis_of(j):
        return (j + core) % 2

    def along(axis):
        return x * (1 - axis) + y * axis

    def h_peer(d):
        return role, (head + d) % 4, ctx

    def block(g):
        return pl.ds(pl.multiple_of(g * ROWS, ROWS), ROWS)

    def slices(slot):
        return pl.ds(pl.multiple_of(slot * 32, 32), 32)

    barrier = pltpu.get_barrier_semaphore()
    peers = [(1 - role, other, ctx) for other in range(4)]
    for d in range(1, 4):
        peers += [peer_of(0, d), peer_of(1, d), h_peer(d)]
    for peer in peers:
        pl.semaphore_signal(barrier, inc=1, device_id=peer, device_id_type=MESH)

    g_copy = pltpu.make_async_copy(gain, g_buf, g_sem)
    x_copies = [pltpu.make_async_copy(hist.at[s], x_buf.at[s], x_sem.at[s]) for s in range(2)]
    w_copies = [
        [pltpu.make_async_copy(w_kv.at[k, :, j], w_buf.at[j, :, k], w_sem.at[j, k]) for k in range(2)]
        for j in range(CHUNKS)
    ]
    q_copies = [pltpu.make_async_copy(quer.at[s], q_buf.at[s], q_sem.at[s]) for s in range(2)]
    wo_copy = pltpu.make_async_copy(w_out, wo_buf, wo_sem)
    g_copy.start()
    x_copies[0].start()
    for copy in w_copies[0]:
        copy.start()

    sends = []

    def send(copies):
        for copy in copies:
            copy.start()
            sends.append(copy)

    def norm(s):
        def rows_of(i, carry):
            rows = pl.ds(i * 64, 64)
            values = x_buf[s, rows, :].astype(jnp.float32)
            mean_sq = jnp.mean(values * values, axis=-1, keepdims=True)
            normed = values * lax.rsqrt(mean_sq + 1e-05) * g_buf[...]
            xn_buf[s, rows, :] = normed.astype(jnp.bfloat16)
            return carry

        lax.fori_loop(0, KEYS // 64, rows_of, 0)

    def kv_copy(s, j, other, slot):
        return pltpu.make_async_remote_copy(
            src_ref=kv_out.at[s, j, other],
            dst_ref=kv_in.at[s, j, :, slices(slot), :],
            send_sem=kv_ss.at[s, j, other],
            recv_sem=kv_rs.at[s, j, slot],
            device_id=(1 - role, other, ctx),
            device_id_type=MESH,
        )

    def send_kv(s, j):
        send([kv_copy(s, j, (head + d) % 4, head) for d in (2, 3, 0, 1)])

    def project(s, chunks):
        for j in chunks:
            if s == 0:
                for copy in w_copies[j]:
                    copy.wait()
            projected = lax.dot_general(
                w_buf[j].reshape(256, D), xn_buf[s], NT, preferred_element_type=jnp.float32
            )
            kv_out[s, j] = projected.astype(jnp.bfloat16).reshape(4, 2, 32, KEYS)
            if s == 0 and j == 0:
                pl.semaphore_wait(barrier, len(peers))
            if CHUNKS * s + j < AHEAD:
                send_kv(s, j)

    g_copy.wait()
    x_copies[0].wait()
    for pair in w_copies[1:]:
        for copy in pair:
            copy.start()
    x_copies[1].start()
    norm(0)
    project(0, (0,))
    q_copies[0].start()
    project(0, (1, 2, 3))
    x_copies[1].wait()
    q_copies[1].start()
    wo_copy.start()
    norm(1)
    project(1, range(CHUNKS))

    ones = jnp.ones((16, KEYS), jnp.bfloat16)

    def a_copies(s, j, d):
        f = (along(axis_of(j)) + d) % 4
        return [
            pltpu.make_async_remote_copy(
                src_ref=src.at[s, j, f],
                dst_ref=dst.at[s, j, d - 1],
                send_sem=a_ss.at[s, j, d - 1, i],
                recv_sem=a_rs.at[s, j, d - 1, i],
                device_id=peer_of(axis_of(j), d),
                device_id_type=MESH,
            )
            for i, (src, dst) in enumerate(((a_out, a_in), (a_ml, a_in_ml)))
        ]

    def b_copies(s, j, d):
        g = (along(1 - axis_of(j)) + d) % 4 // 2
        return [
            pltpu.make_async_remote_copy(
                src_ref=src.at[s, j, g],
                dst_ref=dst.at[s, j, d - 1],
                send_sem=b_ss.at[s, j, d - 1, i],
                recv_sem=b_rs.at[s, j, d - 1, i],
                device_id=peer_of(1 - axis_of(j), d),
                device_id_type=MESH,
            )
            for i, (src, dst) in enumerate(((b_out, b_in), (b_ml, b_in_ml)))
        ]

    def wait_inputs(s, j):
        if j == 0:
            q_copies[s].wait()
        for slot in range(4):
            kv_copy(s, j, slot, slot).wait_recv()

    def attend(s, j):
        keys = kv_in[s, j, 0].T
        values = jnp.concatenate([kv_in[s, j, 1], ones], axis=0)
        columns = slice(j * HD, (j + 1) * HD)
        axis = axis_of(j)
        query_rows = jnp.concatenate(
            [
                q_buf[s, f * axis + g * (1 - axis), f * (1 - axis) + g * axis, :, columns]
                for f in range(4)
                for g in range(4)
            ],
            axis=0,
        )
        scores = lax.dot_general(keys, query_rows, NT, preferred_element_type=jnp.float32)
        peak = jnp.max(scores, axis=0, keepdims=True)
        probability = jnp.exp2((scores - peak) * SCALE).astype(jnp.bfloat16)
        accum = jnp.dot(values, probability, preferred_element_type=jnp.float32)
        for f in range(4):
            lanes = slice(f * KEYS, (f + 1) * KEYS)
            a_out[s, j, f] = accum[:HD, lanes].astype(jnp.bfloat16)
            a_ml[s, j, f, 0:1] = peak[:, lanes]
            a_ml[s, j, f, 1:2] = accum[HD : HD + 1, lanes]

    def merge_first(s, j):
        own = along(axis_of(j))
        parts = [(a_out[s, j, own], a_ml[s, j, own, 0:1], a_ml[s, j, own, 1:2])]
        for d in range(3):
            parts.append((a_in[s, j, d], a_in_ml[s, j, d, 0:1], a_in_ml[s, j, d, 1:2]))
        accum, peak, total = merge(parts)
        accum = accum.astype(jnp.bfloat16)
        for g in range(2):
            lanes = slice(g * HD, (g + 1) * HD)
            b_out[s, j, g] = accum[:, lanes]
            b_ml[s, j, g, 0:1] = peak[:, lanes]
            b_ml[s, j, g, 1:2] = total[:, lanes]

    def merge_second(s, j):
        own = along(1 - axis_of(j)) // 2
        parts = [(b_out[s, j, own], b_ml[s, j, own, 0:1], b_ml[s, j, own, 1:2])]
        for d in range(3):
            parts.append((b_in[s, j, d], b_in_ml[s, j, d, 0:1], b_in_ml[s, j, d, 1:2]))
        accum, _, total = merge(parts)
        t_buf[s, j] = (accum / total).T
        ho_buf[s, :, j * HD : (j + 1) * HD] = t_buf[s, j, block(along(1 - axis_of(j)) % 2), :].astype(jnp.bfloat16)

    def exchange(copies, s, j):
        for d in (2, 1, 3):
            send(copies(s, j, d))

    def arrive(copies, s, j):
        for d in range(1, 4):
            for copy in copies(s, j, d):
                copy.wait_recv()

    def p_copy(s, d):
        return pltpu.make_async_remote_copy(
            src_ref=p_out.at[s, (head + d) % 4],
            dst_ref=p_in.at[s, d - 1],
            send_sem=p_ss.at[s, d - 1],
            recv_sem=p_rs.at[s, d - 1],
            device_id=h_peer(d),
            device_id_type=MESH,
        )

    def finish(s):
        if s == 0:
            wo_copy.wait()
        for other in range(4):
            part = jnp.dot(
                ho_buf[s], wo_buf[:, other * 512 : (other + 1) * 512], preferred_element_type=jnp.float32
            )
            p_out[s, other] = part.astype(jnp.bfloat16)
        send([p_copy(s, d) for d in (2, 1, 3)])

    units = [(s, j) for s in range(2) for j in range(CHUNKS)]

    def step_first(u):
        arrive(a_copies, *units[u])
        merge_first(*units[u])
        exchange(b_copies, *units[u])

    def step_second(u):
        arrive(b_copies, *units[u])
        merge_second(*units[u])

    for u in range(8):
        wait_inputs(*units[u])
        if u + AHEAD < 8:
            send_kv(*units[u + AHEAD])
        attend(*units[u])
        exchange(a_copies, *units[u])
        if u >= 2:
            step_first(u - 2)
        if u >= 4:
            step_second(u - 4)
    finish(0)
    step_first(6)
    step_second(4)
    step_second(5)
    step_first(7)
    step_second(6)
    step_second(7)
    finish(1)
    for s in range(2):
        total = p_out[s, head].astype(jnp.float32)
        for d in range(1, 4):
            p_copy(s, d).wait_recv()
            total = total + p_in[s, d - 1].astype(jnp.float32)
        out[0, s] = total.astype(jnp.bfloat16)
    for copy in sends:
        copy.wait_send()


def local(history, queries, w_kv, gain, w_out):
    bf16, f32 = jnp.bfloat16, jnp.float32
    dma = pltpu.SemaphoreType.DMA
    hist = history.reshape(2, KEYS, D)
    quer = queries.reshape(2, 4, 4, ROWS, 4 * HD)
    w_kv = jnp.transpose(w_kv, (1, 2, 3, 0)).reshape(2, 4, CHUNKS, 32, D)
    return pl.pallas_call(
        kernel,
        out_shape=jax.ShapeDtypeStruct((1, 2, ROWS, 512), bf16),
        in_specs=[pl.BlockSpec(memory_space=pl.ANY)] * 5,
        out_specs=pl.BlockSpec(memory_space=pltpu.VMEM),
        scratch_shapes=[
            pltpu.VMEM((2, KEYS, D), bf16),
            pltpu.VMEM((2, KEYS, D), bf16),
            pltpu.VMEM((1, D), f32),
            pltpu.VMEM((CHUNKS, 4, 2, 32, D), bf16),
            pltpu.VMEM((2, 4, 4, ROWS, 4 * HD), bf16),
            pltpu.VMEM((4 * HD, D), bf16),
            pltpu.VMEM((2, CHUNKS, 4, 2, 32, KEYS), bf16),
            pltpu.VMEM((2, CHUNKS, 2, HD, KEYS), bf16),
            pltpu.VMEM((2, CHUNKS, 4, HD, KEYS), bf16),
            pltpu.VMEM((2, CHUNKS, 4, 2, KEYS), f32),
            pltpu.VMEM((2, CHUNKS, 3, HD, KEYS), bf16),
            pltpu.VMEM((2, CHUNKS, 3, 2, KEYS), f32),
            pltpu.VMEM((2, CHUNKS, 2, HD, HD), bf16),
            pltpu.VMEM((2, CHUNKS, 2, 2, HD), f32),
            pltpu.VMEM((2, CHUNKS, 3, HD, HD), bf16),
            pltpu.VMEM((2, CHUNKS, 3, 2, HD), f32),
            pltpu.VMEM((2, CHUNKS, HD, HD), f32),
            pltpu.VMEM((2, ROWS, 4 * HD), bf16),
            pltpu.VMEM((2, 4, ROWS, 512), bf16),
            pltpu.VMEM((2, 3, ROWS, 512), bf16),
            dma((2,)),
            dma,
            dma((CHUNKS, 2)),
            dma((2,)),
            dma,
            dma((2, CHUNKS, 4)),
            dma((2, CHUNKS, 4)),
            dma((2, CHUNKS, 3, 2)),
            dma((2, CHUNKS, 3, 2)),
            dma((2, CHUNKS, 3, 2)),
            dma((2, CHUNKS, 3, 2)),
            dma((2, 3)),
            dma((2, 3)),
        ],
        compiler_params=pltpu.CompilerParams(
            collective_id=0, has_side_effects=True, vmem_limit_bytes=60 * 2**20
        ),
        cost_estimate=pl.CostEstimate(flops=6 * 10**9, bytes_accessed=10 * 2**20, transcendentals=2**21),
    )(hist, quer, w_kv, gain.reshape(1, D), w_out)


def solution(mesh):
    placed = (
        P("role", None, "ctx", None),
        P("role", None, None, "head"),
        P(None, None, None, "head"),
        P(),
        P("head", None),
    )
    return jax.shard_map(
        local, mesh=mesh, in_specs=placed, out_specs=P("role", None, "ctx", "head"), check_vma=False
    )
```

```python
import math

import jax
import jax.numpy as jnp
from jax import lax
from jax.experimental import pallas as pl
from jax.experimental.pallas import tpu as pltpu
from jax.sharding import PartitionSpec as P

MESH = pl.DeviceIdType.MESH
HD = 128
D = 2048
CHUNKS = 4
KEYS = 256
AHEAD = 2
ROWS = 64
SCALE = math.log2(math.e) / math.sqrt(HD)
NT = (((1,), (1,)), ((), ()))


def merge(parts):
    top = parts[0][1]
    for _, peak, _ in parts[1:]:
        top = jnp.maximum(top, peak)
    accum = total = None
    for part, peak, part_total in parts:
        weight = jnp.exp2((peak - top) * SCALE)
        add = part.astype(jnp.float32) * weight
        accum = add if accum is None else accum + add
        add = part_total * weight
        total = add if total is None else total + add
    return accum, top, total


def kernel(
    hist, quer, w_kv, gain, w_out, out,
    x_buf, xn_buf, g_buf, w_buf, q_buf, wo_buf,
    kv_out, kv_in, a_out, a_ml, a_in, a_in_ml, b_out, b_ml, b_in, b_in_ml,
    t_buf, ho_buf, p_out, p_in,
    x_sem, g_sem, w_sem, q_sem, wo_sem,
    kv_ss, kv_rs, a_ss, a_rs, b_ss, b_rs, p_ss, p_rs,
):
    role, head, ctx = lax.axis_index("role"), lax.axis_index("head"), lax.axis_index("ctx")
    x, y = ctx % 4, ctx // 4
    core = head % 2

    def peer_of(axis, d):
        return role, head, 4 * ((y + d * axis) % 4) + (x + d * (1 - axis)) % 4

    def axis_of(j):
        return (j + core) % 2

    def along(axis):
        return x * (1 - axis) + y * axis

    def h_peer(d):
        return role, (head + d) % 4, ctx

    def block(g):
        return pl.ds(pl.multiple_of(g * ROWS, ROWS), ROWS)

    def slices(slot):
        return pl.ds(pl.multiple_of(slot * 32, 32), 32)

    barrier = pltpu.get_barrier_semaphore()
    peers = [(1 - role, other, ctx) for other in range(4)]
    for d in range(1, 4):
        peers += [peer_of(0, d), peer_of(1, d), h_peer(d)]
    for peer in peers:
        pl.semaphore_signal(barrier, inc=1, device_id=peer, device_id_type=MESH)

    g_copy = pltpu.make_async_copy(gain, g_buf, g_sem)
    x_copies = [pltpu.make_async_copy(hist.at[s], x_buf.at[s], x_sem.at[s]) for s in range(2)]
    w_copies = [
        [pltpu.make_async_copy(w_kv.at[k, :, j], w_buf.at[j, :, k], w_sem.at[j, k]) for k in range(2)]
        for j in range(CHUNKS)
    ]
    q_copies = [pltpu.make_async_copy(quer.at[s], q_buf.at[s], q_sem.at[s]) for s in range(2)]
    wo_copy = pltpu.make_async_copy(w_out, wo_buf, wo_sem)
    g_copy.start()
    x_copies[0].start()
    for copy in w_copies[0]:
        copy.start()

    sends = []

    def send(copies):
        for copy in copies:
            copy.start()
            sends.append(copy)

    def norm(s):
        def rows_of(i, carry):
            rows = pl.ds(i * 64, 64)
            values = x_buf[s, rows, :].astype(jnp.float32)
            mean_sq = jnp.mean(values * values, axis=-1, keepdims=True)
            normed = values * lax.rsqrt(mean_sq + 1e-05) * g_buf[...]
            xn_buf[s, rows, :] = normed.astype(jnp.bfloat16)
            return carry

        lax.fori_loop(0, KEYS // 64, rows_of, 0)

    def kv_copy(s, j, other, slot):
        return pltpu.make_async_remote_copy(
            src_ref=kv_out.at[s, j, other],
            dst_ref=kv_in.at[s, j, :, slices(slot), :],
            send_sem=kv_ss.at[s, j, other],
            recv_sem=kv_rs.at[s, j, slot],
            device_id=(1 - role, other, ctx),
            device_id_type=MESH,
        )

    def send_kv(s, j):
        send([kv_copy(s, j, (head + d) % 4, head) for d in (0, 1, 2, 3)])

    def project(s, chunks):
        for j in chunks:
            if s == 0:
                for copy in w_copies[j]:
                    copy.wait()
            projected = lax.dot_general(
                w_buf[j].reshape(256, D), xn_buf[s], NT, preferred_element_type=jnp.float32
            )
            kv_out[s, j] = projected.astype(jnp.bfloat16).reshape(4, 2, 32, KEYS)
            if s == 0 and j == 0:
                pl.semaphore_wait(barrier, len(peers))
            if CHUNKS * s + j < AHEAD:
                send_kv(s, j)

    g_copy.wait()
    x_copies[0].wait()
    for pair in w_copies[1:]:
        for copy in pair:
            copy.start()
    x_copies[1].start()
    norm(0)
    project(0, (0,))
    q_copies[0].start()
    project(0, (1, 2, 3))
    x_copies[1].wait()
    q_copies[1].start()
    wo_copy.start()
    norm(1)
    project(1, range(CHUNKS))

    ones = jnp.ones((16, KEYS), jnp.bfloat16)

    def a_copies(s, j, d):
        f = (along(axis_of(j)) + d) % 4
        return [
            pltpu.make_async_remote_copy(
                src_ref=src.at[s, j, f],
                dst_ref=dst.at[s, j, d - 1],
                send_sem=a_ss.at[s, j, d - 1, i],
                recv_sem=a_rs.at[s, j, d - 1, i],
                device_id=peer_of(axis_of(j), d),
                device_id_type=MESH,
            )
            for i, (src, dst) in enumerate(((a_out, a_in), (a_ml, a_in_ml)))
        ]

    def b_copies(s, j, d):
        g = (along(1 - axis_of(j)) + d) % 4 // 2
        return [
            pltpu.make_async_remote_copy(
                src_ref=src.at[s, j, g],
                dst_ref=dst.at[s, j, d - 1],
                send_sem=b_ss.at[s, j, d - 1, i],
                recv_sem=b_rs.at[s, j, d - 1, i],
                device_id=peer_of(1 - axis_of(j), d),
                device_id_type=MESH,
            )
            for i, (src, dst) in enumerate(((b_out, b_in), (b_ml, b_in_ml)))
        ]

    def wait_inputs(s, j):
        if j == 0:
            q_copies[s].wait()
        for slot in range(4):
            kv_copy(s, j, slot, slot).wait_recv()

    def attend(s, j):
        keys = kv_in[s, j, 0].T
        values = jnp.concatenate([kv_in[s, j, 1], ones], axis=0)
        columns = slice(j * HD, (j + 1) * HD)
        axis = axis_of(j)
        query_rows = jnp.concatenate(
            [
                q_buf[s, f * axis + g * (1 - axis), f * (1 - axis) + g * axis, :, columns]
                for f in range(4)
                for g in range(4)
            ],
            axis=0,
        )
        scores = lax.dot_general(keys, query_rows, NT, preferred_element_type=jnp.float32)
        peak = jnp.max(scores, axis=0, keepdims=True)
        probability = jnp.exp2((scores - peak) * SCALE).astype(jnp.bfloat16)
        accum = jnp.dot(values, probability, preferred_element_type=jnp.float32)
        for f in range(4):
            lanes = slice(f * KEYS, (f + 1) * KEYS)
            a_out[s, j, f] = accum[:HD, lanes].astype(jnp.bfloat16)
            a_ml[s, j, f, 0:1] = peak[:, lanes]
            a_ml[s, j, f, 1:2] = accum[HD : HD + 1, lanes]

    def merge_first(s, j):
        own = along(axis_of(j))
        parts = [(a_out[s, j, own], a_ml[s, j, own, 0:1], a_ml[s, j, own, 1:2])]
        for d in range(3):
            parts.append((a_in[s, j, d], a_in_ml[s, j, d, 0:1], a_in_ml[s, j, d, 1:2]))
        accum, peak, total = merge(parts)
        accum = accum.astype(jnp.bfloat16)
        for g in range(2):
            lanes = slice(g * HD, (g + 1) * HD)
            b_out[s, j, g] = accum[:, lanes]
            b_ml[s, j, g, 0:1] = peak[:, lanes]
            b_ml[s, j, g, 1:2] = total[:, lanes]

    def merge_second(s, j):
        own = along(1 - axis_of(j)) // 2
        parts = [(b_out[s, j, own], b_ml[s, j, own, 0:1], b_ml[s, j, own, 1:2])]
        for d in range(3):
            parts.append((b_in[s, j, d], b_in_ml[s, j, d, 0:1], b_in_ml[s, j, d, 1:2]))
        accum, _, total = merge(parts)
        t_buf[s, j] = (accum / total).T
        ho_buf[s, :, j * HD : (j + 1) * HD] = t_buf[s, j, block(along(1 - axis_of(j)) % 2), :].astype(jnp.bfloat16)

    def exchange(copies, s, j):
        for d in (2, 1, 3):
            send(copies(s, j, d))

    def arrive(copies, s, j):
        for d in range(1, 4):
            for copy in copies(s, j, d):
                copy.wait_recv()

    def p_copy(s, d):
        return pltpu.make_async_remote_copy(
            src_ref=p_out.at[s, (head + d) % 4],
            dst_ref=p_in.at[s, d - 1],
            send_sem=p_ss.at[s, d - 1],
            recv_sem=p_rs.at[s, d - 1],
            device_id=h_peer(d),
            device_id_type=MESH,
        )

    def finish(s):
        if s == 0:
            wo_copy.wait()
        for other in range(4):
            part = jnp.dot(
                ho_buf[s], wo_buf[:, other * 512 : (other + 1) * 512], preferred_element_type=jnp.float32
            )
            p_out[s, other] = part.astype(jnp.bfloat16)
        send([p_copy(s, d) for d in (2, 1, 3)])

    units = [(s, j) for s in range(2) for j in range(CHUNKS)]

    def step_first(u):
        arrive(a_copies, *units[u])
        merge_first(*units[u])
        exchange(b_copies, *units[u])

    def step_second(u):
        arrive(b_copies, *units[u])
        merge_second(*units[u])

    for u in range(8):
        wait_inputs(*units[u])
        if u + AHEAD < 8:
            send_kv(*units[u + AHEAD])
        attend(*units[u])
        exchange(a_copies, *units[u])
        if u >= 2:
            step_first(u - 2)
        if u >= 4:
            step_second(u - 4)
    finish(0)
    step_first(6)
    step_second(4)
    step_second(5)
    step_first(7)
    step_second(6)
    step_second(7)
    finish(1)
    for s in range(2):
        total = p_out[s, head].astype(jnp.float32)
        for d in range(1, 4):
            p_copy(s, d).wait_recv()
            total = total + p_in[s, d - 1].astype(jnp.float32)
        out[0, s] = total.astype(jnp.bfloat16)
    for copy in sends:
        copy.wait_send()


def local(history, queries, w_kv, gain, w_out):
    bf16, f32 = jnp.bfloat16, jnp.float32
    dma = pltpu.SemaphoreType.DMA
    hist = history.reshape(2, KEYS, D)
    quer = queries.reshape(2, 4, 4, ROWS, 4 * HD)
    w_kv = jnp.transpose(w_kv, (1, 2, 3, 0)).reshape(2, 4, CHUNKS, 32, D)
    return pl.pallas_call(
        kernel,
        out_shape=jax.ShapeDtypeStruct((1, 2, ROWS, 512), bf16),
        in_specs=[pl.BlockSpec(memory_space=pl.ANY)] * 5,
        out_specs=pl.BlockSpec(memory_space=pltpu.VMEM),
        scratch_shapes=[
            pltpu.VMEM((2, KEYS, D), bf16),
            pltpu.VMEM((2, KEYS, D), bf16),
            pltpu.VMEM((1, D), f32),
            pltpu.VMEM((CHUNKS, 4, 2, 32, D), bf16),
            pltpu.VMEM((2, 4, 4, ROWS, 4 * HD), bf16),
            pltpu.VMEM((4 * HD, D), bf16),
            pltpu.VMEM((2, CHUNKS, 4, 2, 32, KEYS), bf16),
            pltpu.VMEM((2, CHUNKS, 2, HD, KEYS), bf16),
            pltpu.VMEM((2, CHUNKS, 4, HD, KEYS), bf16),
            pltpu.VMEM((2, CHUNKS, 4, 2, KEYS), f32),
            pltpu.VMEM((2, CHUNKS, 3, HD, KEYS), bf16),
            pltpu.VMEM((2, CHUNKS, 3, 2, KEYS), f32),
            pltpu.VMEM((2, CHUNKS, 2, HD, HD), bf16),
            pltpu.VMEM((2, CHUNKS, 2, 2, HD), f32),
            pltpu.VMEM((2, CHUNKS, 3, HD, HD), bf16),
            pltpu.VMEM((2, CHUNKS, 3, 2, HD), f32),
            pltpu.VMEM((2, CHUNKS, HD, HD), f32),
            pltpu.VMEM((2, ROWS, 4 * HD), bf16),
            pltpu.VMEM((2, 4, ROWS, 512), bf16),
            pltpu.VMEM((2, 3, ROWS, 512), bf16),
            dma((2,)),
            dma,
            dma((CHUNKS, 2)),
            dma((2,)),
            dma,
            dma((2, CHUNKS, 4)),
            dma((2, CHUNKS, 4)),
            dma((2, CHUNKS, 3, 2)),
            dma((2, CHUNKS, 3, 2)),
            dma((2, CHUNKS, 3, 2)),
            dma((2, CHUNKS, 3, 2)),
            dma((2, 3)),
            dma((2, 3)),
        ],
        compiler_params=pltpu.CompilerParams(
            collective_id=0, has_side_effects=True, vmem_limit_bytes=60 * 2**20
        ),
        cost_estimate=pl.CostEstimate(flops=6 * 10**9, bytes_accessed=10 * 2**20, transcendentals=2**21),
    )(hist, quer, w_kv, gain.reshape(1, D), w_out)


def solution(mesh):
    placed = (
        P("role", None, "ctx", None),
        P("role", None, None, "head"),
        P(None, None, None, "head"),
        P(),
        P("head", None),
    )
    return jax.shard_map(
        local, mesh=mesh, in_specs=placed, out_specs=P("role", None, "ctx", "head"), check_vma=False
    )
```
